256 devices in a mesh: outer: 8 (over y, x_lo), inner: 32 (over x_hi, z, core).
Axes of the slice: x: 4 (x_hi: 2, x_lo: 2; x = x_hi * 2 + x_lo), y: 4, z: 8, core: 2. Of those that a mesh axis runs over, the one named last changes fastest.
Arguments:
- volume: bfloat16 [4, 128, 128, 1024], P(None, 'outer', 'inner'), may hold values from -6 to 6
- cotangent: bfloat16 [4, 128, 128, 1024], P(None, 'outer', 'inner'), may hold values from -6 to 6
- gain_width: bfloat16 [1024], replicated, may hold values from 0.25 to 1.75
- qkv_width: bfloat16 [1024, 1536], replicated, may hold values from -5 to 5
- out_width: bfloat16 [512, 1024], replicated, may hold values from -0.25 to 0.25
- gain_height: bfloat16 [1024], replicated, may hold values from 0.25 to 1.75
- qkv_height: bfloat16 [1024, 1536], replicated, may hold values from -5 to 5
- out_height: bfloat16 [512, 1024], replicated, may hold values from -0.25 to 0.25
Outputs:
- result: bfloat16 [4, 128, 128, 1024], P(None, 'outer', 'inner')
- volume_grad: bfloat16 [4, 128, 128, 1024], P(None, 'outer', 'inner')
The draws below stay inside these ranges and needn't reach their ends.
All inputs are finite; a program needn't handle non-finite values.
Results may differ from the reference program's by a relative error of at most 0.015.
Values may be sent and summed in bfloat16 or wider, within the bound.
A program may use at most 64 MiB of HBM per device.

```python
import jax
import jax.numpy as jnp
from jax import lax

D = 1024
HEADS = 8
T_SIZE = 4
INNER = 512
H = 128
W = 128


def projection_matrix(key):
    base = jax.random.normal(key, (D, 3 * INNER), jnp.float32) * D ** (-0.5)
    return base.astype(jnp.bfloat16)


def draw_qkv_width(key, part):
    key = jax.random.fold_in(key, 11)
    return projection_matrix(key)


def draw_qkv_height(key, part):
    key = jax.random.fold_in(key, 23)
    return projection_matrix(key)


def levels(rng, dims, shards, low, largest):
    def one(position, shards_of):
        steps = jax.random.uniform(jax.random.fold_in(jax.random.fold_in(rng, 6), position), (shards_of,), jnp.float32, low / len(shards), largest / len(shards))
        return jnp.repeat(jnp.exp(steps), dims[position] // shards_of).reshape((-1,) + (1,) * (len(dims) - position - 1))

    level = one(*shards[0])
    for cut in shards[1:]:
        level = level * one(*cut)
    return level


def noise(key, shape, deviation, limit, pieces=(), dtype=jnp.bfloat16):
    level = levels(key, shape, pieces, -0.22, 0.18) if pieces else 1.0
    entries = jax.random.normal(key, shape, jnp.float32) * deviation * level
    return jnp.minimum(jnp.maximum(entries, -limit), limit).astype(dtype)


def setup_inputs(seed: int = 0) -> dict:
    streams_of = jax.random.split(jax.random.key(seed), 9)
    return {
        "volume": noise(streams_of[0], (T_SIZE, H, W, D), 1.0, 6.0, ((1, 8), (2, 32))),
        "cotangent": noise(streams_of[1], (T_SIZE, H, W, D), 1.0, 6.0, ((1, 8), (2, 32))),
        "gain_width": jnp.clip(1.0 + 0.15 * jax.random.normal(streams_of[2], (D,), jnp.float32), 0.25, 1.75).astype(jnp.bfloat16),
        "qkv_width": draw_qkv_width(jax.random.fold_in(streams_of[8], 71), 0),
        "out_width": noise(streams_of[4], (INNER, D), INNER ** -0.5, 0.25),
        "gain_height": jnp.clip(1.0 + 0.15 * jax.random.normal(streams_of[5], (D,), jnp.float32), 0.25, 1.75).astype(jnp.bfloat16),
        "qkv_height": draw_qkv_height(jax.random.fold_in(streams_of[8], 71), 0),
        "out_height": noise(streams_of[7], (INNER, D), INNER ** -0.5, 0.25),
    }


def sublayer(rows, gain, qkv, out):
    lines, length, width = rows.shape
    inner = out.shape[0]
    heads = HEADS
    hdim = inner // heads
    values32 = rows.astype(jnp.float32)
    meansq = lax.optimization_barrier(jnp.mean(values32 * values32, axis=-1, keepdims=True))
    normed = (values32 * lax.rsqrt(meansq + 1e-06) * gain.astype(jnp.float32)).astype(jnp.bfloat16)
    proj = jnp.dot(normed.reshape(lines * length, width), qkv, preferred_element_type=jnp.float32).astype(jnp.bfloat16)
    proj = proj.reshape(lines, length, 3, heads, hdim)
    query = proj[:, :, 0]
    keys = proj[:, :, 1]
    vals = proj[:, :, 2]
    scores = jnp.einsum('rqhd,rkhd->rhqk', query, keys, preferred_element_type=jnp.float32) * 0.125
    top = lax.optimization_barrier(jnp.max(scores, axis=-1, keepdims=True))
    expo = jnp.exp(scores - top)
    probs = (expo / lax.optimization_barrier(jnp.sum(expo, axis=-1, keepdims=True))).astype(jnp.bfloat16)
    mixed = jnp.einsum('rhqk,rkhd->rqhd', probs, vals, preferred_element_type=jnp.float32).astype(jnp.bfloat16)
    mixed = mixed.reshape(lines * length, inner)
    branch = jnp.dot(mixed, out, preferred_element_type=jnp.float32).reshape(lines, length, width)
    return (values32 + branch).astype(jnp.bfloat16)

def apply_lines(rows, params, block):
    lines, length, width = rows.shape
    grouped = rows.reshape(lines // block, block, length, width)
    done = lax.map(lambda part: sublayer(part, *params), grouped)
    return done.reshape(lines, length, width)

def grad_lines(rows, cot, params, block):
    lines, length, width = rows.shape
    grouped = rows.reshape(lines // block, block, length, width)
    cots = cot.reshape(lines // block, block, length, width)

    def one(pair):
        pullback = jax.vjp(lambda part: sublayer(part, *params), pair[0])[1]
        return pullback(pair[1])[0]
    done = lax.map(one, (grouped, cots))
    return done.reshape(lines, length, width)

def reference(volume, cotangent, gain_width, qkv_width, out_width, gain_height, qkv_height, out_height):
    frames, rows_h, cols_w, width = volume.shape
    pw = (gain_width, qkv_width, out_width)
    ph = (gain_height, qkv_height, out_height)
    along_w = volume.reshape(frames * rows_h, cols_w, width)
    middle = apply_lines(along_w, pw, frames).reshape(frames, rows_h, cols_w, width)
    along_h = middle.transpose(0, 2, 1, 3).reshape(frames * cols_w, rows_h, width)
    done_h = apply_lines(along_h, ph, frames)
    result = done_h.reshape(frames, cols_w, rows_h, width).transpose(0, 2, 1, 3)
    cot_h = cotangent.transpose(0, 2, 1, 3).reshape(frames * cols_w, rows_h, width)
    middle_grad = grad_lines(along_h, cot_h, ph, frames)
    middle_grad = middle_grad.reshape(frames, cols_w, rows_h, width).transpose(0, 2, 1, 3)
    volume_grad = grad_lines(along_w, middle_grad.reshape(frames * rows_h, cols_w, width), pw, frames)
    return (result, volume_grad.reshape(frames, rows_h, cols_w, width))
```

```python
import jax
import jax.numpy as jnp
from jax import lax
from jax.experimental import pallas as pl
from jax.experimental.pallas import tpu as pltpu
from jax.sharding import PartitionSpec as P

MESH = pl.DeviceIdType.MESH
BF = jnp.bfloat16
F32 = jnp.float32
D = 1024
INNER = 512
NI = 32
NO = 8
TOK = 256
PAIRS = 4
EPS = 1e-06


def dot(a, b):
    return jnp.dot(a, b, preferred_element_type=F32)


def dot_nt(a, b):
    return lax.dot_general(a, b, (((1,), (1,)), ((), ())), preferred_element_type=F32)


def dot_tn(a, b):
    return lax.dot_general(a, b, (((0,), (0,)), ((), ())), preferred_element_type=F32)


def home_to_height(r):
    return (r // 64) * 64 + (r % 16) * 4 + (r // 16) % 4


def arrive_to_lines(r):
    return ((r // 4) % 32) * 8 + (r // 128) * 4 + r % 4


def lines_to_pack(r):
    return ((r // 2) % 2) * 128 + (r // 8) * 4 + ((r // 4) % 2) * 2 + r % 2


def pack_to_height(r):
    return (r % 128) * 2 + r // 128


def one_hot(order, inverse):
    row = lax.broadcasted_iota(jnp.int32, (TOK, TOK), 0)
    col = lax.broadcasted_iota(jnp.int32, (TOK, TOK), 1)
    hit = (row == order(col)) if inverse else (col == order(row))
    return jnp.where(hit, 1.0, 0.0).astype(BF)


def low_rows(shape):
    return lax.broadcasted_iota(jnp.int32, shape, 0) % 8 < 4


def pack_wide(rows):
    g = rows.reshape(NI, 8, D)
    return jnp.concatenate([g[:, :, : D // 2], g[:, :, D // 2 :]], axis=1).reshape(2 * TOK, D // 2).astype(BF)


def unpack_wide(buf):
    g = buf.astype(F32).reshape(NI, 16, D // 2)
    return jnp.concatenate([g[:, :8], g[:, 8:]], axis=2).reshape(TOK, D)


def pack_narrow(rows):
    m = [rows[:, 128 * q : 128 * q + 128] for q in range(4)]
    low = low_rows((TOK, 128))
    parts = [
        jnp.where(low, m[0], pltpu.roll(m[1], 4, 0)),
        jnp.where(low, m[2], pltpu.roll(m[3], 4, 0)),
        jnp.where(low, pltpu.roll(m[0], TOK - 4, 0), m[1]),
        jnp.where(low, pltpu.roll(m[2], TOK - 4, 0), m[3]),
    ]
    return jnp.stack([p.reshape(32, 8, 128) for p in parts], axis=1).reshape(1024, 128).astype(BF)


def unpack_narrow(buf):
    g = buf.astype(F32).reshape(32, 4, 8, 128)
    v = [g[:, q].reshape(TOK, 128) for q in range(4)]
    low = low_rows((TOK, 128))
    return jnp.concatenate(
        [
            jnp.where(low, v[0], pltpu.roll(v[2], 4, 0)),
            jnp.where(low, pltpu.roll(v[0], TOK - 4, 0), v[2]),
            jnp.where(low, v[1], pltpu.roll(v[3], 4, 0)),
            jnp.where(low, pltpu.roll(v[1], TOK - 4, 0), v[3]),
        ],
        axis=1,
    )


def scale_of(v):
    return lax.rsqrt(jnp.mean(v * v, axis=-1, keepdims=True) + EPS)


def norm_back(v, dn, gain, resid):
    r = scale_of(v)
    gd = dn * gain
    c = jnp.sum(gd * v, axis=-1, keepdims=True) * (1.0 / D)
    return r * gd - v * (r * r * r * c) + resid


def lane_low():
    return lax.broadcasted_iota(jnp.int32, (128, 128), 1) < 64


def two_heads(a):
    low = lane_low()
    zero = jnp.zeros_like(a)
    return jnp.concatenate([jnp.where(low, a, zero), jnp.where(low, zero, a)], axis=0)


def one_pair(a):
    return jnp.where(lane_low(), a[:128], a[128:])


def unit_slices(line, pair):
    rows = pl.ds(line * 128, 128)
    return rows, [pl.ds(INNER * part + 128 * pair, 128) for part in range(3)]


def attend(proj, probs, mixed):
    for line in range(2):
        for pair in range(PAIRS):
            rows, (qs, ks, vs) = unit_slices(line, pair)
            s = dot_nt(two_heads(proj[rows, qs]), proj[rows, ks]) * 0.125
            e = jnp.exp(s - jnp.max(s, axis=-1, keepdims=True))
            p = e / jnp.sum(e, axis=-1, keepdims=True)
            probs[line * PAIRS + pair] = p
            mixed[rows, pl.ds(128 * pair, 128)] = one_pair(dot(p.astype(BF), proj[rows, vs])).astype(BF)


def attend_back(proj, probs, dmixed, dproj):
    for line in range(2):
        for pair in range(PAIRS):
            rows, (qs, ks, vs) = unit_slices(line, pair)
            p = probs[line * PAIRS + pair]
            do = two_heads(dmixed[rows, pl.ds(128 * pair, 128)])
            dp = dot_nt(do, proj[rows, vs]).astype(BF).astype(F32)
            dproj[rows, vs] = dot_tn(p.astype(BF), do).astype(BF)
            ds = p * (dp - jnp.sum(dp * p, axis=-1, keepdims=True)) * 0.125
            ds = ds.astype(BF)
            dproj[rows, qs] = one_pair(dot(ds, proj[rows, ks])).astype(BF)
            dproj[rows, ks] = dot_tn(ds, two_heads(proj[rows, qs])).astype(BF)


def far_first(k):
    return (4 + (1 - 2 * (k % 2)) * ((k + 1) // 2)) % 8


def kernel(
    vol_ref, cot_ref, gw_ref, gh_ref, qkvw_hbm, outw_hbm, qkvh_hbm, outh_hbm,
    res_ref, grad_ref,
    qkvw, outw, qkvh, outh, perms,
    s1, r1, s2, r2, s3, r3, s4, r4,
    sx, rx, sc, rc, sres, rres, smg, rmg,
    proj, projh, probs, probsh, mixed, mixedh, dproj, dmix, dmixh, mid,
    load_sem, send_sem, recv_sem, local_sem,
):
    i = lax.axis_index("inner")
    o = lax.axis_index("outer")
    ix, iz, ic = i // 16, (i // 2) % 8, i % 2
    oy, ol = o // 2, o % 2
    frame_w = ix * 2 + iz % 2
    slot_w = (iz // 2) * 2 + ic
    frame_h = (oy + iz) % 4
    same = frame_w == frame_h

    def device_of(f, j):
        return (f // 2) * 16 + ((j // 2) * 2 + f % 2) * 2 + j % 2

    def block_of(d):
        return (((d // 16) * 2 + (d // 2) % 2) * 8) + ((d // 4) % 4) * 2 + d % 2

    loads = [
        pltpu.make_async_copy(a, b, load_sem.at[n])
        for n, (a, b) in enumerate(((qkvw_hbm, qkvw), (outh_hbm, outh), (outw_hbm, outw), (qkvh_hbm, qkvh)))
    ]
    for load in loads:
        load.start()

    barrier = pltpu.get_barrier_semaphore()

    def greet_inner(k, c):
        pl.semaphore_signal(barrier, inc=1, device_id={"inner": (i + k) % NI}, device_id_type=MESH)
        return c

    def greet_outer(k, c):
        pl.semaphore_signal(barrier, inc=1, device_id={"outer": (o + k) % NO}, device_id_type=MESH)
        return c

    lax.fori_loop(1, NI, greet_inner, 0)
    lax.fori_loop(1, NO, greet_outer, 0)

    def rows16(b, n=1):
        return pl.ds(pl.multiple_of(b * 16, 16), 16 * n)

    def remote(src, dst, phase, target):
        return pltpu.make_async_remote_copy(
            src_ref=src, dst_ref=dst, send_sem=send_sem.at[phase], recv_sem=recv_sem.at[phase],
            device_id=target, device_id_type=MESH,
        )

    def all_inner(src, dst, phase, src_block, my_block):
        def go(k, c):
            dz = far_first(k // 2 % 8)
            dx = 1 - k // 16
            dc = 1 - k % 2
            d = ((ix + dx) % 2) * 16 + ((iz + dz) % 8) * 2 + (ic + dc) % 2
            remote(src.at[rows16(src_block(d))], dst.at[rows16(my_block)], phase, {"inner": d}).start()
            return c

        lax.fori_loop(0, NI - 1, go, 0)
        dst[rows16(my_block)] = src[rows16(src_block(i))]

    def height_line(p):
        return 2 * ((p // 2 + iz) % 4) + p % 2

    def to_height(src, dst, phase):
        def go(k, c):
            p = (o + k) % NO
            remote(
                src.at[pl.ds(height_line(p) * 2, 2)], dst.at[:, rows16(o), :], phase, {"outer": p}
            ).start()
            return c

        lax.fori_loop(1, NO, go, 0)
        dst[:, rows16(o), :] = src[pl.ds(height_line(o) * 2, 2)]

    def from_height(src, dst, phase):
        def go(k, c):
            p = (o + k) % NO
            remote(
                src.at[:, rows16(p), :], dst.at[pl.ds(height_line(o) * 2, 2)], phase, {"outer": p}
            ).start()
            return c

        lax.fori_loop(1, NO, go, 0)
        dst[pl.ds(height_line(o) * 2, 2)] = src[:, rows16(o), :]

    def wait_bytes(part, sem):
        pltpu.make_async_copy(part, part, sem).wait()

    def wait_cross(buf, sem):
        @pl.when(same)
        def _():
            wait_bytes(buf.at[pl.ds(0, 63 * 16)], sem)

        @pl.when(jnp.logical_not(same))
        def _():
            wait_bytes(buf, sem)

    wait_wide = lambda buf, sem: wait_bytes(buf.at[pl.ds(0, 31 * 16)], sem)
    wait_outer = lambda buf, sem: wait_bytes(buf.at[pl.ds(0, 14)], sem)

    gain_w = gw_ref[...].astype(F32)
    gain_h = gh_ref[...].astype(F32)
    x = vol_ref[...].astype(F32).reshape(TOK, D)
    s1[...] = pack_wide(x * scale_of(x) * gain_w)
    pl.semaphore_wait(barrier, NI + NO - 2)
    all_inner(s1, r1, 0, block_of, i)

    perms[0] = one_hot(home_to_height, False)
    sx[...] = dot(perms[0], x.astype(BF)).astype(BF).reshape(16, 16, D)
    to_height(sx, rx, 1)
    cot = cot_ref[...].astype(F32).reshape(TOK, D).astype(BF)
    sc[...] = dot(perms[0], cot).astype(BF).reshape(16, 16, D)
    to_height(sc, rc, 2)
    for n, (order, inverse) in enumerate((
        (home_to_height, True), (arrive_to_lines, False), (arrive_to_lines, True), (lines_to_pack, False),
        (lines_to_pack, True), (pack_to_height, False), (pack_to_height, True),
    )):
        perms[n + 1] = one_hot(order, inverse)
    loads[0].wait()
    loads[1].wait()

    wait_wide(r1, recv_sem.at[0])
    lines = dot(perms[2], unpack_wide(r1[...]).astype(BF)).astype(BF)
    proj[...] = dot(lines, qkvw[...]).astype(BF)
    attend(proj, probs, mixed)
    s2[...] = pack_narrow(dot(perms[4], mixed[...]))

    def cross_out(k, c):
        e = k % 2
        kk = k // 2
        dx = 1 - kk // 16
        dz = far_first(kk // 2 % 8)
        dc = 1 - kk % 2
        s = ((ix + dx) % 2) * 16 + ((iz + dz) % 8) * 2 + (ic + dc) % 2
        p = ((frame_w - (s // 2) % 8 + 8) % 4) * 2 + e
        mine = jnp.logical_and(s == i, p == o)
        src = s2.at[rows16(2 * s + e)]
        dst = r2.at[rows16(o * 8 + slot_w)]

        @pl.when(jnp.logical_not(mine))
        def _():
            remote(src, dst, 3, {"outer": p, "inner": s}).start()

        @pl.when(mine)
        def _():
            copy = pltpu.make_async_copy(src, dst, local_sem)
            copy.start()
            copy.wait()

        return c

    lax.fori_loop(0, 64, cross_out, 0)

    loads[2].wait()
    loads[3].wait()
    wait_bytes(rx.at[:, pl.ds(0, 112), :], recv_sem.at[1])
    wait_bytes(rc.at[:, pl.ds(0, 112), :], recv_sem.at[2])
    coth = rc[...].reshape(TOK, D)
    dmixh[...] = dot_nt(coth, outh[...]).astype(BF)

    wait_cross(r2, recv_sem.at[3])
    mixed_here = dot(perms[6], unpack_narrow(r2[...]).astype(BF)).astype(BF)
    middle = (rx[...].reshape(TOK, D).astype(F32) + dot(mixed_here, outw[...])).astype(BF)
    mid[...] = middle
    m32 = middle.astype(F32)
    normed = (m32 * scale_of(m32) * gain_h).astype(BF)
    projh[...] = dot(normed, qkvh[...]).astype(BF)
    attend(projh, probsh, mixedh)
    attend_back(projh, probsh, dmixh, dproj)
    dn = dot_nt(dproj[...], qkvh[...]).astype(BF).astype(F32)
    mgrad = norm_back(mid[...].astype(F32), dn, gain_h, rc[...].reshape(TOK, D).astype(F32)).astype(BF)
    smg[...] = mgrad.reshape(2, 128, D)
    dmw = dot_nt(mgrad, outw[...]).astype(BF)
    s3[...] = pack_narrow(dot(perms[7], dmw))

    def cross_back(k, c):
        p = (o + 7 - k // 8) % 8
        j = (slot_w + k % 8) % 8
        d = device_of(frame_h, j)
        mine = jnp.logical_and(p == o, d == i)
        src = s3.at[rows16(p * 8 + j)]
        dst = r3.at[rows16(2 * i + ol)]

        @pl.when(jnp.logical_not(mine))
        def _():
            remote(src, dst, 4, {"outer": p, "inner": d}).start()

        @pl.when(mine)
        def _():
            copy = pltpu.make_async_copy(src, dst, local_sem)
            copy.start()
            copy.wait()

        return c

    lax.fori_loop(0, 64, cross_back, 0)

    from_height(smg, rmg, 5)
    sres[...] = (mid[...].astype(F32) + dot(mixedh[...], outh[...])).astype(BF).reshape(2, 128, D)
    from_height(sres, rres, 6)

    wait_cross(r3, recv_sem.at[4])
    dmix[...] = dot(perms[5], unpack_narrow(r3[...]).astype(BF)).astype(BF)
    attend_back(proj, probs, dmix, dproj)
    dnw = dot_nt(dproj[...], qkvw[...]).astype(BF)
    s4[...] = pack_wide(dot(perms[3], dnw))
    all_inner(s4, r4, 7, lambda d: d, block_of(i))

    wait_outer(rres, recv_sem.at[6])
    res_ref[...] = dot(perms[1], rres[...].reshape(TOK, D)).reshape(64, 4, D).astype(BF)
    wait_outer(rmg, recv_sem.at[5])
    resid = dot(perms[1], rmg[...].reshape(TOK, D))
    wait_wide(r4, recv_sem.at[7])
    x = vol_ref[...].astype(F32).reshape(TOK, D)
    grad_ref[...] = norm_back(x, unpack_wide(r4[...]), gain_w, resid).reshape(64, 4, D).astype(BF)

    wait_wide(s1, send_sem.at[0])
    wait_outer(sx, send_sem.at[1])
    wait_outer(sc, send_sem.at[2])
    wait_cross(s2, send_sem.at[3])
    wait_cross(s3, send_sem.at[4])
    wait_bytes(smg.at[:, pl.ds(0, 112), :], send_sem.at[5])
    wait_bytes(sres.at[:, pl.ds(0, 112), :], send_sem.at[6])
    wait_wide(s4, send_sem.at[7])


def on_device(volume, cotangent, gain_width, qkv_width, out_width, gain_height, qkv_height, out_height):
    shape = volume.shape
    vm = pl.BlockSpec(memory_space=pltpu.VMEM)
    hbm = pl.BlockSpec(memory_space=pl.ANY)
    flat = jax.ShapeDtypeStruct((64, 4, D), BF)
    v = lambda *s: pltpu.VMEM(s, BF)
    result, grad = pl.pallas_call(
        kernel,
        out_shape=(flat, flat),
        in_specs=[vm, vm, vm, vm, hbm, hbm, hbm, hbm],
        out_specs=(vm, vm),
        scratch_shapes=[
            v(D, 3 * INNER), v(INNER, D), v(D, 3 * INNER), v(INNER, D), v(8, TOK, TOK),
            v(512, 512), v(512, 512), v(1024, 128), v(1024, 128), v(1024, 128), v(1024, 128), v(512, 512), v(512, 512),
            v(16, 16, D), v(2, 128, D), v(16, 16, D), v(2, 128, D),
            v(2, 128, D), v(16, 16, D), v(2, 128, D), v(16, 16, D),
            v(TOK, 3 * INNER), v(TOK, 3 * INNER), pltpu.VMEM((8, TOK, 128), F32), pltpu.VMEM((8, TOK, 128), F32),
            v(TOK, INNER), v(TOK, INNER), v(TOK, 3 * INNER), v(TOK, INNER), v(TOK, INNER), v(TOK, D),
            pltpu.SemaphoreType.DMA((4,)), pltpu.SemaphoreType.DMA((8,)), pltpu.SemaphoreType.DMA((8,)),
            pltpu.SemaphoreType.DMA,
        ],
        compiler_params=pltpu.CompilerParams(
            collective_id=0, has_side_effects=True, vmem_limit_bytes=60 * 1024 * 1024
        ),
    )(
        volume.reshape(64, 4, D), cotangent.reshape(64, 4, D), gain_width.reshape(1, D), gain_height.reshape(1, D),
        qkv_width, out_width, qkv_height, out_height,
    )
    return result.reshape(shape), grad.reshape(shape)


def solution(mesh):
    split = P(None, "outer", "inner", None)
    return jax.shard_map(
        on_device,
        mesh=mesh,
        in_specs=(split, split, P(), P(), P(), P(), P(), P()),
        out_specs=(split, split),
        check_vma=False,
    )
```

```python
import jax
import jax.numpy as jnp
from jax import lax
from jax.experimental import pallas as pl
from jax.experimental.pallas import tpu as pltpu
from jax.sharding import PartitionSpec as P

MESH = pl.DeviceIdType.MESH
BF = jnp.bfloat16
F32 = jnp.float32
D = 1024
INNER = 512
NI = 32
NO = 8
TOK = 256
PAIRS = 4
EPS = 1e-06


def dot(a, b):
    return jnp.dot(a, b, preferred_element_type=F32)


def dot_nt(a, b):
    return lax.dot_general(a, b, (((1,), (1,)), ((), ())), preferred_element_type=F32)


def dot_tn(a, b):
    return lax.dot_general(a, b, (((0,), (0,)), ((), ())), preferred_element_type=F32)


def home_to_height(r):
    return (r // 64) * 64 + ((r % 8) * 2 + (r // 8) % 2) * 4 + (r // 16) % 4


def height_to_home(r):
    return (r // 64) * 64 + (r % 4) * 16 + ((r // 4) % 2) * 8 + (r // 8) % 8


def last_to_first(r):
    return (r % 64) * 2 + r // 64


def first_to_last(r):
    return (r % 2) * 64 + r // 2


def back_to_lines(r):
    return (r % 2) * 128 + ((r // 2) % 64) * 2 + r // 128


def one_hot(order, n):
    row = lax.broadcasted_iota(jnp.int32, (n, n), 0)
    col = lax.broadcasted_iota(jnp.int32, (n, n), 1)
    return jnp.where(col == order(row), 1.0, 0.0).astype(BF)


def in_low(shape, size):
    return (lax.broadcasted_iota(jnp.int32, shape, 1) // size) % 2 == 0


def swap(a, b, size):
    low = in_low(a.shape, size)
    return jnp.where(low, a, pltpu.roll(b, size, 1)), jnp.where(low, pltpu.roll(a, 8 - size, 1), b)


def pack_tokens(rows):
    g = rows.reshape(rows.shape[0] // 8, 8, D)
    return swap(g[:, :, : D // 2], g[:, :, D // 2 :], 4)


def unpack_tokens(a, b):
    a, b = swap(a, b, 4)
    return jnp.concatenate([a, b], axis=2).reshape(a.shape[0] * 8, D)


def turn(q):
    a0, a2 = swap(q[0], q[2], 4)
    a1, a3 = swap(q[1], q[3], 4)
    return swap(a0, a1, 2) + swap(a2, a3, 2)


def pack_pairs(rows):
    g = rows.reshape(16, 8, INNER)
    parts = turn([g[:, :, 128 * q : 128 * q + 128] for q in range(4)])
    return jnp.stack(parts, axis=1).reshape(64, 8, 128).astype(BF)


def unpack_pairs(blocks):
    g = blocks.astype(F32).reshape(16, 4, 8, 128)
    return jnp.concatenate(turn([g[:, q] for q in range(4)]), axis=2).reshape(128, INNER).astype(BF)


def scale_of(v):
    return lax.rsqrt(jnp.mean(v * v, axis=-1, keepdims=True) + EPS)


def norm_back(v, dn, gain, resid):
    r = scale_of(v)
    gd = dn * gain
    c = jnp.sum(gd * v, axis=-1, keepdims=True) * (1.0 / D)
    return r * gd - v * (r * r * r * c) + resid


def lane_low():
    return lax.broadcasted_iota(jnp.int32, (128, 128), 1) < 64


def two_heads(a):
    low = lane_low()
    zero = jnp.zeros_like(a)
    return jnp.concatenate([jnp.where(low, a, zero), jnp.where(low, zero, a)], axis=0)


def one_pair(a):
    return jnp.where(lane_low(), a[:128], a[128:])


def unit_slices(line, pair):
    rows = pl.ds(line * 128, 128)
    return rows, [pl.ds(INNER * part + 128 * pair, 128) for part in range(3)]


def attend(proj, probs, mixed, line):
    for pair in range(PAIRS):
        rows, (qs, ks, vs) = unit_slices(line, pair)
        s = dot_nt(two_heads(proj[rows, qs]), proj[rows, ks]) * 0.125
        e = jnp.exp(s - jnp.max(s, axis=-1, keepdims=True))
        p = e / jnp.sum(e, axis=-1, keepdims=True)
        probs[line * PAIRS + pair] = p
        mixed[rows, pl.ds(128 * pair, 128)] = one_pair(dot(p.astype(BF), proj[rows, vs])).astype(BF)


def attend_back(proj, probs, dmixed, dproj, line):
    for pair in range(PAIRS):
        rows, (qs, ks, vs) = unit_slices(line, pair)
        p = probs[line * PAIRS + pair]
        do = two_heads(dmixed[rows, pl.ds(128 * pair, 128)])
        dp = dot_nt(do, proj[rows, vs]).astype(BF).astype(F32)
        dproj[rows, vs] = dot_tn(p.astype(BF), do).astype(BF)
        ds = p * (dp - jnp.sum(dp * p, axis=-1, keepdims=True)) * 0.125
        ds = ds.astype(BF)
        dproj[rows, qs] = one_pair(dot(ds, proj[rows, ks])).astype(BF)
        dproj[rows, ks] = dot_tn(ds, two_heads(proj[rows, qs])).astype(BF)


FAR_FIRST = (4, 3, 5, 2, 6, 1, 7, 0)


def kernel(
    vol_ref, cot_ref, gw_ref, gh_ref, qkvw_hbm, outw_hbm, qkvh_hbm, outh_hbm,
    res_ref, grad_ref,
    qkvw, outw, qkvh, outh, perms, halves,
    s1, r1, s2, r2, s3, r3, s4, r4,
    sx, rx, sc, rc, sres, rres, smg, rmg,
    proj, projh, probs, probsh, mixed, mixedh, dproj, dmix, dmixh, mid,
    load_sem, send_sem, recv_sem, local_sem,
):
    i = lax.axis_index("inner")
    o = lax.axis_index("outer")
    ix, iz, ic = i // 16, (i // 2) % 8, i % 2
    oy, ol = o // 2, o % 2
    frame_w = ix * 2 + iz % 2
    slot_w = (iz // 2) * 2 + ic
    frame_h = (oy + iz) % 4
    same = frame_w == frame_h
    xs = (ix, (ix + 1) % 2)
    zs = [(iz + d) % 8 for d in range(8)]
    cs = (ic, (ic + 1) % 2)

    loads = [
        pltpu.make_async_copy(a, b, load_sem.at[n])
        for n, (a, b) in enumerate(((qkvw_hbm, qkvw), (outh_hbm, outh), (outw_hbm, outw), (qkvh_hbm, qkvh)))
    ]
    for load in loads:
        load.start()

    barrier = pltpu.get_barrier_semaphore()

    def greet_inner(k, c):
        pl.semaphore_signal(barrier, inc=1, device_id={"inner": (i + k) % NI}, device_id_type=MESH)
        return c

    def greet_outer(k, c):
        pl.semaphore_signal(barrier, inc=1, device_id={"outer": (o + k) % NO}, device_id_type=MESH)
        return c

    lax.fori_loop(1, NI, greet_inner, 0)
    lax.fori_loop(1, NO, greet_outer, 0)

    def remote(src, dst, sem, target):
        pltpu.make_async_remote_copy(
            src_ref=src, dst_ref=dst, send_sem=send_sem.at[sem], recv_sem=recv_sem.at[sem],
            device_id=target, device_id_type=MESH,
        ).start()

    def local(src, dst):
        copy = pltpu.make_async_copy(src, dst, local_sem)
        copy.start()
        copy.wait()

    def block(x, z, c):
        return (x * 2 + z % 2) * 8 + (z // 2) * 2 + c

    def to_width(half):
        for dx in (1, 0):
            for dz in FAR_FIRST:
                for dc in (1, 0):
                    x, z, c = xs[dx], zs[dz], cs[dc]
                    src, dst = s1.at[half, block(x, z, c)], r1.at[half, i]
                    if dx or dz or dc:
                        remote(src, dst, half, {"inner": x * 16 + z * 2 + c})
                    else:
                        local(src, dst)

    def from_width(half):
        for dx in (1, 0):
            for dz in FAR_FIRST:
                for dc in (1, 0):
                    d = xs[dx] * 16 + zs[dz] * 2 + cs[dc]
                    src, dst = s4.at[half, d], r4.at[half, block(ix, iz, ic)]
                    if dx or dz or dc:
                        remote(src, dst, 6 + half, {"inner": d})
                    else:
                        local(src, dst)

    def width_to_height(half):
        for dx in (1, 0):
            for dz in FAR_FIRST:
                y = (frame_w + 8 - zs[dz]) % 4
                for dc in (1, 0):
                    for e in (0, 1):
                        s = xs[dx] * 16 + zs[dz] * 2 + cs[dc]
                        p = y * 2 + e
                        src, dst = s2.at[half, 2 * s + e], r2.at[half, o * 8 + slot_w]
                        if dx or dz or dc:
                            remote(src, dst, 2 + half, {"outer": p, "inner": s})
                        else:
                            pl.when(p != o)(lambda src=src, dst=dst, p=p, s=s: remote(src, dst, 2 + half, {"outer": p, "inner": s}))
                            pl.when(p == o)(lambda src=src, dst=dst: local(src, dst))

    def height_to_width(half):
        base = (frame_h // 2) * 16 + (frame_h % 2) * 2
        js = [(slot_w + k) % 8 for k in range(8)]
        ds = [base + (j // 2) * 4 + j % 2 for j in js]
        for dp in (7, 6, 5, 4, 3, 2, 1, 0):
            p = (o + dp) % 8
            for k in range(8):
                src, dst = s3.at[half, p * 8 + js[k]], r3.at[half, 2 * i + ol]
                if dp or k:
                    remote(src, dst, 4 + half, {"outer": p, "inner": ds[k]})
                else:
                    pl.when(ds[k] != i)(lambda src=src, dst=dst, p=p, d=ds[k]: remote(src, dst, 4 + half, {"outer": p, "inner": d}))
                    pl.when(ds[k] == i)(lambda src=src, dst=dst: local(src, dst))

    def height_line(p):
        return 2 * ((p // 2 + iz) % 4) + p % 2

    def to_height(src, dst, sem):
        def go(k, c):
            p = (o + k) % NO
            remote(src.at[pl.ds(height_line(p) * 2, 2)], dst.at[:, :, o], sem, {"outer": p})
            return c

        lax.fori_loop(1, NO, go, 0)
        local(src.at[pl.ds(height_line(o) * 2, 2)], dst.at[:, :, o])

    def from_height(src, dst, sem):
        def go(k, c):
            p = (o + k) % NO
            remote(src.at[:, :, p], dst.at[pl.ds(height_line(o) * 2, 2)], sem, {"outer": p})
            return c

        lax.fori_loop(1, NO, go, 0)
        local(src.at[:, :, o], dst.at[pl.ds(height_line(o) * 2, 2)])

    def wait_bytes(part, sem):
        pltpu.make_async_copy(part, part, sem).wait()

    def wait_inner(buf, half, sem):
        wait_bytes(buf.at[half, pl.ds(0, 31)], sem)

    def wait_cross(buf, half, sem):
        pl.when(same)(lambda: wait_bytes(buf.at[half, pl.ds(0, 63)], sem))
        pl.when(jnp.logical_not(same))(lambda: wait_bytes(buf.at[half], sem))

    def wait_lines(buf, sem):
        wait_bytes(buf.at[:, :, pl.ds(0, 7)], sem)

    def wait_home(buf, sem):
        wait_bytes(buf.at[pl.ds(0, 14)], sem)

    gain_w = gw_ref[...].astype(F32).reshape(1, D)
    gain_h = gh_ref[...].astype(F32).reshape(1, D)
    x = vol_ref[...].astype(F32).reshape(TOK, D)
    first, second = pack_tokens(x * scale_of(x) * gain_w)
    s1[0] = first.astype(BF)
    s1[1] = second.astype(BF)
    pl.semaphore_wait(barrier, NI + NO - 2)
    to_width(0)
    to_width(1)

    perms[0] = one_hot(home_to_height, TOK)
    sx[...] = dot(perms[0], x.astype(BF)).astype(BF).reshape(16, 2, 8, D)
    to_height(sx, rx, 8)
    cot = cot_ref[...].astype(F32).reshape(TOK, D).astype(BF)
    sc[...] = dot(perms[0], cot).astype(BF).reshape(16, 2, 8, D)
    to_height(sc, rc, 9)
    perms[1] = one_hot(height_to_home, TOK)
    perms[2] = one_hot(back_to_lines, TOK)
    halves[0] = one_hot(last_to_first, 128)
    halves[1] = one_hot(first_to_last, 128)
    loads[0].wait()
    loads[1].wait()

    for line in range(2):
        rows = pl.ds(line * 128, 128)
        wait_inner(r1, line, recv_sem.at[line])
        got = r1[line].astype(F32).reshape(16, 2, 8, D // 2)
        tokens = unpack_tokens(got[:, 0], got[:, 1]).astype(BF)
        proj[rows] = dot(tokens, qkvw[...]).astype(BF)
        attend(proj, probs, mixed, line)
        s2[line] = pack_pairs(mixed[rows].astype(F32))
        width_to_height(line)

    loads[2].wait()
    loads[3].wait()
    wait_lines(rx, recv_sem.at[8])
    wait_lines(rc, recv_sem.at[9])
    dmixh[...] = dot_nt(rc[...].reshape(TOK, D), outh[...]).astype(BF)

    for half in range(2):
        wait_cross(r2, half, recv_sem.at[2 + half])
        here = dot(halves[0], unpack_pairs(r2[half])).astype(BF)
        middle = (rx[:, half].astype(F32).reshape(128, D) + dot(here, outw[...])).astype(BF)
        m32 = middle.astype(F32)
        normed = (m32 * scale_of(m32) * gain_h).astype(BF)
        got = dot(normed, qkvh[...]).astype(BF)
        for line in range(2):
            rows = pl.ds(line * 128 + half * 64, 64)
            mid[rows] = middle[line * 64 : line * 64 + 64]
            projh[rows] = got[line * 64 : line * 64 + 64]
    for line in range(2):
        rows = pl.ds(line * 128, 128)
        attend(projh, probsh, mixedh, line)
        attend_back(projh, probsh, dmixh, dproj, line)
        dn = dot_nt(dproj[rows], qkvh[...]).astype(BF).astype(F32)
        resid = rc[line].astype(F32).reshape(128, D)
        mgrad = norm_back(mid[rows].astype(F32), dn, gain_h, resid).astype(BF)
        smg[line] = mgrad.reshape(2, 8, 8, D)
        dmw = dot_nt(mgrad, outw[...]).astype(BF)
        s3[line] = pack_pairs(dot(halves[1], dmw))
        height_to_width(line)
    from_height(smg, rmg, 10)
    sres[...] = (mid[...].astype(F32) + dot(mixedh[...], outh[...])).astype(BF).reshape(2, 2, 8, 8, D)
    from_height(sres, rres, 11)

    wait_cross(r3, 0, recv_sem.at[4])
    wait_cross(r3, 1, recv_sem.at[5])
    back = jnp.concatenate([unpack_pairs(r3[0]), unpack_pairs(r3[1])], axis=0)
    dmix[...] = dot(perms[2], back).astype(BF)
    for line in range(2):
        rows = pl.ds(line * 128, 128)
        attend_back(proj, probs, dmix, dproj, line)
        dn = dot_nt(dproj[rows], qkvw[...]).astype(BF).astype(F32)
        s4[line] = jnp.stack(pack_tokens(dn), axis=1).reshape(NI, 8, D // 2).astype(BF)
        from_width(line)

    wait_home(rres, recv_sem.at[11])
    res_ref[...] = dot(perms[1], rres[...].reshape(TOK, D)).reshape(64, 4, D).astype(BF)
    wait_home(rmg, recv_sem.at[10])
    resid = dot(perms[1], rmg[...].reshape(TOK, D))
    wait_inner(r4, 0, recv_sem.at[6])
    wait_inner(r4, 1, recv_sem.at[7])
    x = vol_ref[...].astype(F32).reshape(TOK, D)
    dn = unpack_tokens(r4[0].astype(F32), r4[1].astype(F32))
    grad_ref[...] = norm_back(x, dn, gain_w, resid).reshape(64, 4, D).astype(BF)

    for half in range(2):
        wait_inner(s1, half, send_sem.at[half])
        wait_cross(s2, half, send_sem.at[2 + half])
        wait_cross(s3, half, send_sem.at[4 + half])
        wait_inner(s4, half, send_sem.at[6 + half])
    wait_home(sx, send_sem.at[8])
    wait_home(sc, send_sem.at[9])
    wait_lines(smg, send_sem.at[10])
    wait_lines(sres, send_sem.at[11])


def hand_over(a_ref, b_ref, x_ref, y_ref):
    x_ref[...] = a_ref[...]
    y_ref[...] = b_ref[...]


def on_device(volume, cotangent, gain_width, qkv_width, out_width, gain_height, qkv_height, out_height):
    shape = volume.shape
    vm = pl.BlockSpec(memory_space=pltpu.VMEM)
    hbm = pl.BlockSpec(memory_space=pl.ANY)
    flat = jax.ShapeDtypeStruct((64, 4, D), BF)
    v = lambda *s: pltpu.VMEM(s, BF)
    result, grad = pl.pallas_call(
        kernel,
        out_shape=(flat, flat),
        in_specs=[vm, vm, vm, vm, hbm, hbm, hbm, hbm],
        out_specs=(vm, vm),
        scratch_shapes=[
            v(D, 3 * INNER), v(INNER, D), v(D, 3 * INNER), v(INNER, D), v(3, TOK, TOK), v(2, 128, 128),
            v(2, 32, 8, 512), v(2, 32, 8, 512), v(2, 64, 8, 128), v(2, 64, 8, 128),
            v(2, 64, 8, 128), v(2, 64, 8, 128), v(2, 32, 8, 512), v(2, 32, 8, 512),
            v(16, 2, 8, D), v(2, 2, 8, 8, D), v(16, 2, 8, D), v(2, 2, 8, 8, D),
            v(2, 2, 8, 8, D), v(16, 2, 8, D), v(2, 2, 8, 8, D), v(16, 2, 8, D),
            v(TOK, 3 * INNER), v(TOK, 3 * INNER), pltpu.VMEM((8, TOK, 128), F32), pltpu.VMEM((8, TOK, 128), F32),
            v(TOK, INNER), v(TOK, INNER), v(TOK, 3 * INNER), v(TOK, INNER), v(TOK, INNER), v(TOK, D),
            pltpu.SemaphoreType.DMA((4,)), pltpu.SemaphoreType.DMA((12,)), pltpu.SemaphoreType.DMA((12,)),
            pltpu.SemaphoreType.DMA,
        ],
        compiler_params=pltpu.CompilerParams(
            collective_id=0, has_side_effects=True, vmem_limit_bytes=60 * 1024 * 1024
        ),
    )(
        volume.reshape(64, 4, D), cotangent.reshape(64, 4, D), gain_width, gain_height,
        qkv_width, out_width, qkv_height, out_height,
    )
    result, grad = pl.pallas_call(hand_over, out_shape=(flat, flat), in_specs=[vm, vm], out_specs=(vm, vm))(result, grad)
    return result.reshape(shape), grad.reshape(shape)


def solution(mesh):
    split = P(None, "outer", "inner", None)
    return jax.shard_map(
        on_device,
        mesh=mesh,
        in_specs=(split, split, P(), P(), P(), P(), P(), P()),
        out_specs=(split, split),
        check_vma=False,
    )
```

```python
import jax
import jax.numpy as jnp
from jax import lax
from jax.experimental import pallas as pl
from jax.experimental.pallas import tpu as pltpu
from jax.sharding import PartitionSpec as P

MESH = pl.DeviceIdType.MESH
BF = jnp.bfloat16
F32 = jnp.float32
D = 1024
INNER = 512
NI = 32
NO = 8
TOK = 256
PAIRS = 4
EPS = 1e-06


def dot(a, b):
    return jnp.dot(a, b, preferred_element_type=F32)


def dot_nt(a, b):
    return lax.dot_general(a, b, (((1,), (1,)), ((), ())), preferred_element_type=F32)


def dot_tn(a, b):
    return lax.dot_general(a, b, (((0,), (0,)), ((), ())), preferred_element_type=F32)


def home_to_height(r):
    return (r // 64) * 64 + ((r % 8) * 2 + (r // 8) % 2) * 4 + (r // 16) % 4


def height_to_home(r):
    return (r // 64) * 64 + (r % 4) * 16 + ((r // 4) % 2) * 8 + (r // 8) % 8


def last_to_first(r):
    return (r % 64) * 2 + r // 64


def back_to_lines(r):
    return ((r // 2) % 64) * 4 + (r // 128) * 2 + r % 2


def lines_to_back(r):
    return (r % 2) * 128 + ((r // 2) % 2) * 64 + r // 4


def one_hot(order, n):
    row = lax.broadcasted_iota(jnp.int32, (n, n), 0)
    col = lax.broadcasted_iota(jnp.int32, (n, n), 1)
    return jnp.where(col == order(row), 1.0, 0.0).astype(BF)


def in_low(shape, size):
    return (lax.broadcasted_iota(jnp.int32, shape, 1) // size) % 2 == 0


def swap(a, b, size):
    low = in_low(a.shape, size)
    return jnp.where(low, a, pltpu.roll(b, size, 1)), jnp.where(low, pltpu.roll(a, 8 - size, 1), b)


def pack_tokens(rows):
    g = rows.reshape(rows.shape[0] // 8, 8, D)
    return swap(g[:, :, : D // 2], g[:, :, D // 2 :], 4)


def unpack_tokens(a, b):
    a, b = swap(a, b, 4)
    return jnp.concatenate([a, b], axis=2).reshape(a.shape[0] * 8, D)


def turn(q):
    a0, a2 = swap(q[0], q[2], 4)
    a1, a3 = swap(q[1], q[3], 4)
    return swap(a0, a1, 2) + swap(a2, a3, 2)


def pack_pairs(rows):
    g = rows.reshape(16, 8, INNER)
    parts = turn([g[:, :, 128 * q : 128 * q + 128] for q in range(4)])
    return jnp.stack(parts, axis=1).reshape(64, 8, 128).astype(BF)


def unpack_pairs(blocks):
    g = blocks.astype(F32).reshape(16, 4, 8, 128)
    return jnp.concatenate(turn([g[:, q] for q in range(4)]), axis=2).reshape(128, INNER).astype(BF)


def pack_fours(rows):
    g = rows.reshape(32, 8, INNER)
    q = [g[:, :, 128 * k : 128 * k + 128] for k in range(4)]
    (a0, b0), (a1, b1) = swap(q[0], q[1], 4), swap(q[2], q[3], 4)
    return jnp.stack((a0, a1, b0, b1), axis=1).reshape(64, 16, 128).astype(BF)


def unpack_fours(blocks):
    g = blocks.astype(F32).reshape(32, 4, 8, 128)
    parts = swap(g[:, 0], g[:, 2], 4) + swap(g[:, 1], g[:, 3], 4)
    return jnp.concatenate(parts, axis=2).reshape(TOK, INNER).astype(BF)


def scale_of(v):
    return lax.rsqrt(jnp.mean(v * v, axis=-1, keepdims=True) + EPS)


def norm_back(v, dn, gain, resid):
    r = scale_of(v)
    gd = dn * gain
    c = jnp.sum(gd * v, axis=-1, keepdims=True) * (1.0 / D)
    return r * gd - v * (r * r * r * c) + resid


def lane_low():
    return lax.broadcasted_iota(jnp.int32, (128, 128), 1) < 64


def two_heads(a):
    low = lane_low()
    zero = jnp.zeros_like(a)
    return jnp.concatenate([jnp.where(low, a, zero), jnp.where(low, zero, a)], axis=0)


def one_pair(a):
    return jnp.where(lane_low(), a[:128], a[128:])


def unit_slices(line, pair):
    rows = pl.ds(line * 128, 128)
    return rows, [pl.ds(INNER * part + 128 * pair, 128) for part in range(3)]


def attend(proj, probs, mixed, line):
    for pair in range(PAIRS):
        rows, (qs, ks, vs) = unit_slices(line, pair)
        s = dot_nt(two_heads(proj[rows, qs]), proj[rows, ks]) * 0.125
        e = jnp.exp(s - jnp.max(s, axis=-1, keepdims=True))
        p = e * (1.0 / jnp.sum(e, axis=-1, keepdims=True))
        probs[line * PAIRS + pair] = p
        mixed[rows, pl.ds(128 * pair, 128)] = one_pair(dot(p.astype(BF), proj[rows, vs])).astype(BF)


def attend_back(proj, probs, dmixed, dproj, line):
    for pair in range(PAIRS):
        rows, (qs, ks, vs) = unit_slices(line, pair)
        p = probs[line * PAIRS + pair]
        do = two_heads(dmixed[rows, pl.ds(128 * pair, 128)])
        dp = dot_nt(do, proj[rows, vs]).astype(BF).astype(F32)
        dproj[rows, vs] = dot_tn(p.astype(BF), do).astype(BF)
        ds = p * (dp - jnp.sum(dp * p, axis=-1, keepdims=True)) * 0.125
        ds = ds.astype(BF)
        dproj[rows, qs] = one_pair(dot(ds, proj[rows, ks])).astype(BF)
        dproj[rows, ks] = dot_tn(ds, two_heads(proj[rows, qs])).astype(BF)


FAR_FIRST = (4, 3, 5, 2, 6, 1, 7, 0)


def kernel(
    vol_hbm, cot_hbm, gw_hbm, gh_hbm, qkvw_hbm, outw_hbm, qkvh_hbm, outh_hbm,
    res_hbm, grad_hbm,
    vol_ref, cot_ref, res_ref, grad_ref, gw_ref, gh_ref, qkvw, outw, qkvh, outh, perms, halves,
    s1, r1, s2, r2, s3, r3, s4, r4,
    sx, rx, sc, rc, sres, rres, smg, rmg,
    proj, projh, probs, probsh, mixed, mixedh, dproj, dmix, dmixh, mid,
    load_sem, store_sem, send_sem, recv_sem, local_sem,
):
    i = lax.axis_index("inner")
    o = lax.axis_index("outer")
    ix, iz, ic = i // 16, (i // 2) % 8, i % 2
    oy, ol = o // 2, o % 2
    frame_w = (iz % 2) * 2 + ix
    slot_w = (iz // 2) * 2 + ic
    frame_h = (oy + iz) % 4
    same = frame_w == frame_h
    xs = (ix, (ix + 1) % 2)
    zs = [(iz + d) % 8 for d in range(8)]
    cs = (ic, (ic + 1) % 2)

    barrier = pltpu.get_barrier_semaphore()
    for dx in (1, 0):
        for dz in FAR_FIRST:
            for dc in (1, 0):
                if dx or dz or dc:
                    greeted = {"inner": xs[dx] * 16 + zs[dz] * 2 + cs[dc]}
                    pl.semaphore_signal(barrier, inc=1, device_id=greeted, device_id_type=MESH)
    for dp in range(1, NO):
        pl.semaphore_signal(barrier, inc=1, device_id={"outer": (o + dp) % NO}, device_id_type=MESH)

    moves = ((vol_hbm, vol_ref), (cot_hbm, cot_ref), (qkvw_hbm, qkvw), (outh_hbm, outh), (outw_hbm, outw), (qkvh_hbm, qkvh), (gw_hbm, gw_ref), (gh_hbm, gh_ref))
    loads = [pltpu.make_async_copy(a, b, load_sem.at[n]) for n, (a, b) in enumerate(moves)]
    for n in (0, 6, 7, 1, 2, 3, 4, 5):
        loads[n].start()

    def remote(src, dst, sem, target):
        pltpu.make_async_remote_copy(
            src_ref=src, dst_ref=dst, send_sem=send_sem.at[sem], recv_sem=recv_sem.at[sem],
            device_id=target, device_id_type=MESH,
        ).start()

    def local(src, dst):
        copy = pltpu.make_async_copy(src, dst, local_sem)
        copy.start()
        copy.wait()

    def block(x, z, c):
        return ((z % 2) * 2 + x) * 8 + (z // 2) * 2 + c

    def to_width():
        for odd in (0, 1):
            turned = (iz + odd) % 2
            far = [(iz + a + turned * (b - a)) % 8 for a, b in ((4, 3), (2, 5), (6, 1), (0, 7))]
            for half in (0, 1):
                for dx in (1, 0):
                    for k, z in enumerate(far):
                        for dc in (1, 0):
                            x, c = xs[dx], cs[dc]
                            src, dst = s1.at[half, block(x, z, c)], r1.at[half, i]
                            send = lambda src=src, dst=dst, d=x * 16 + z * 2 + c, half=half: remote(src, dst, half, {"inner": d})
                            if dx or dc or k < 3:
                                send()
                            else:
                                pl.when(turned != 0)(send)
                                pl.when(turned == 0)(lambda src=src, dst=dst: local(src, dst))

    def from_width(half):
        for dx in (1, 0):
            for dz in FAR_FIRST:
                for dc in (1, 0):
                    d = xs[dx] * 16 + zs[dz] * 2 + cs[dc]
                    src, dst = s4.at[half, d], r4.at[half, block(ix, iz, ic)]
                    if dx or dz or dc:
                        remote(src, dst, 6 + half, {"inner": d})
                    else:
                        local(src, dst)

    def width_to_height(half):
        for dx in (1, 0):
            for dz in FAR_FIRST:
                y = (frame_w + 8 - zs[dz]) % 4
                for dc in (1, 0):
                    for e in (0, 1):
                        s = xs[dx] * 16 + zs[dz] * 2 + cs[dc]
                        p = y * 2 + e
                        src, dst = s2.at[half, 2 * s + e], r2.at[half, o * 8 + slot_w]
                        if dx or dz or dc:
                            remote(src, dst, 2 + half, {"outer": p, "inner": s})
                        else:
                            pl.when(p != o)(lambda src=src, dst=dst, p=p, s=s: remote(src, dst, 2 + half, {"outer": p, "inner": s}))
                            pl.when(p == o)(lambda src=src, dst=dst: local(src, dst))

    def height_to_width():
        base = (frame_h % 2) * 16 + (frame_h // 2) * 2
        js = [(slot_w + k) % 8 for k in range(8)]
        ds = [base + (j // 2) * 4 + j % 2 for j in js]
        for dp in (7, 6, 5, 4, 3, 2, 1, 0):
            p = (o + dp) % 8
            for k in range(8):
                src, dst = s3.at[p * 8 + js[k]], r3.at[2 * i + ol]
                if dp or k:
                    remote(src, dst, 4, {"outer": p, "inner": ds[k]})
                else:
                    pl.when(ds[k] != i)(lambda src=src, dst=dst, p=p, d=ds[k]: remote(src, dst, 4, {"outer": p, "inner": d}))
                    pl.when(ds[k] == i)(lambda src=src, dst=dst: local(src, dst))

    def height_line(p):
        return 2 * ((p // 2 + iz) % 4) + p % 2

    def to_height(src, dst, sem):
        def go(k, c):
            p = (o + k) % NO
            remote(src.at[pl.ds(height_line(p) * 2, 2)], dst.at[:, :, o], sem, {"outer": p})
            return c

        lax.fori_loop(1, NO, go, 0)
        local(src.at[pl.ds(height_line(o) * 2, 2)], dst.at[:, :, o])

    def from_height(src, dst, sem):
        def go(k, c):
            p = (o + k) % NO
            remote(src.at[:, :, p], dst.at[pl.ds(height_line(o) * 2, 2)], sem, {"outer": p})
            return c

        lax.fori_loop(1, NO, go, 0)
        local(src.at[:, :, o], dst.at[pl.ds(height_line(o) * 2, 2)])

    def wait_bytes(part, sem):
        pltpu.make_async_copy(part, part, sem).wait()

    def wait_inner(buf, half, sem):
        wait_bytes(buf.at[half, pl.ds(0, 31)], sem)

    def wait_back(buf, sem):
        pl.when(same)(lambda: wait_bytes(buf.at[pl.ds(0, 63)], sem))
        pl.when(jnp.logical_not(same))(lambda: wait_bytes(buf, sem))

    def wait_cross(buf, half, sem):
        pl.when(same)(lambda: wait_bytes(buf.at[half, pl.ds(0, 63)], sem))
        pl.when(jnp.logical_not(same))(lambda: wait_bytes(buf.at[half], sem))

    def wait_lines(buf, sem):
        wait_bytes(buf.at[:, :, pl.ds(0, 7)], sem)

    def wait_home(buf, sem):
        wait_bytes(buf.at[pl.ds(0, 14)], sem)

    loads[6].wait()
    loads[7].wait()
    gain_w = gw_ref[...].astype(F32).reshape(1, D)
    gain_h = gh_ref[...].astype(F32).reshape(1, D)
    loads[0].wait()
    x = vol_ref[...].astype(F32).reshape(TOK, D)
    first, second = pack_tokens(x * scale_of(x) * gain_w)
    s1[0] = first.astype(BF)
    s1[1] = second.astype(BF)
    pl.semaphore_wait(barrier, NI + NO - 2)
    to_width()

    perms[0] = one_hot(home_to_height, TOK)
    sx[...] = dot(perms[0], x.astype(BF)).astype(BF).reshape(16, 2, 8, D)
    to_height(sx, rx, 8)
    loads[1].wait()
    cot = cot_ref[...].astype(F32).reshape(TOK, D).astype(BF)
    sc[...] = dot(perms[0], cot).astype(BF).reshape(16, 2, 8, D)
    to_height(sc, rc, 9)
    perms[1] = one_hot(height_to_home, TOK)
    perms[2] = one_hot(back_to_lines, TOK)
    halves[...] = one_hot(last_to_first, 128)
    perms[3] = one_hot(lines_to_back, TOK)
    loads[2].wait()
    loads[3].wait()

    for line in range(2):
        rows = pl.ds(line * 128, 128)
        wait_inner(r1, line, recv_sem.at[line])
        got = r1[line].astype(F32).reshape(16, 2, 8, D // 2)
        tokens = unpack_tokens(got[:, 0], got[:, 1]).astype(BF)
        proj[rows] = dot(tokens, qkvw[...]).astype(BF)
        attend(proj, probs, mixed, line)
        s2[line] = pack_pairs(mixed[rows].astype(F32))
        width_to_height(line)

    loads[4].wait()
    loads[5].wait()
    wait_lines(rx, recv_sem.at[8])
    wait_lines(rc, recv_sem.at[9])
    dmixh[...] = dot_nt(rc[...].reshape(TOK, D), outh[...]).astype(BF)

    for half in range(2):
        wait_cross(r2, half, recv_sem.at[2 + half])
        here = dot(halves[...], unpack_pairs(r2[half])).astype(BF)
        middle = (rx[:, half].astype(F32).reshape(128, D) + dot(here, outw[...])).astype(BF)
        m32 = middle.astype(F32)
        normed = (m32 * scale_of(m32) * gain_h).astype(BF)
        got = dot(normed, qkvh[...]).astype(BF)
        for line in range(2):
            rows = pl.ds(line * 128 + half * 64, 64)
            mid[rows] = middle[line * 64 : line * 64 + 64]
            projh[rows] = got[line * 64 : line * 64 + 64]
    for line in range(2):
        attend(projh, probsh, mixedh, line)
        attend_back(projh, probsh, dmixh, dproj, line)
    dn = dot_nt(dproj[...], qkvh[...]).astype(BF).astype(F32)
    mgrad = norm_back(mid[...].astype(F32), dn, gain_h, rc[...].astype(F32).reshape(TOK, D)).astype(BF)
    smg[...] = mgrad.reshape(2, 2, 8, 8, D)
    dmw = dot_nt(mgrad, outw[...]).astype(BF)
    s3[...] = pack_fours(dot(perms[3], dmw))
    height_to_width()
    from_height(smg, rmg, 10)
    sres[...] = (mid[...].astype(F32) + dot(mixedh[...], outh[...])).astype(BF).reshape(2, 2, 8, 8, D)
    from_height(sres, rres, 11)

    wait_back(r3, recv_sem.at[4])
    dmix[...] = dot(perms[2], unpack_fours(r3[...])).astype(BF)
    for line in range(2):
        rows = pl.ds(line * 128, 128)
        attend_back(proj, probs, dmix, dproj, line)
        dn = dot_nt(dproj[rows], qkvw[...]).astype(BF).astype(F32)
        s4[line] = jnp.stack(pack_tokens(dn), axis=1).reshape(NI, 8, D // 2).astype(BF)
        from_width(line)

    wait_home(rres, recv_sem.at[11])
    res_ref[...] = dot(perms[1], rres[...].reshape(TOK, D)).reshape(64, 4, D).astype(BF)
    stores = [
        pltpu.make_async_copy(a, b, store_sem.at[n])
        for n, (a, b) in enumerate(((res_ref, res_hbm), (grad_ref, grad_hbm)))
    ]
    stores[0].start()
    wait_home(rmg, recv_sem.at[10])
    resid = dot(perms[1], rmg[...].reshape(TOK, D))
    wait_inner(r4, 0, recv_sem.at[6])
    wait_inner(r4, 1, recv_sem.at[7])
    x = vol_ref[...].astype(F32).reshape(TOK, D)
    dn = unpack_tokens(r4[0].astype(F32), r4[1].astype(F32))
    grad_ref[...] = norm_back(x, dn, gain_w, resid).reshape(64, 4, D).astype(BF)
    stores[1].start()

    for half in range(2):
        wait_inner(s1, half, send_sem.at[half])
        wait_cross(s2, half, send_sem.at[2 + half])
        wait_inner(s4, half, send_sem.at[6 + half])
    wait_back(s3, send_sem.at[4])
    wait_home(sx, send_sem.at[8])
    wait_home(sc, send_sem.at[9])
    wait_lines(smg, send_sem.at[10])
    wait_lines(sres, send_sem.at[11])
    stores[0].wait()
    stores[1].wait()


def hand_over(a_hbm, b_hbm, x_hbm, y_hbm, a, b, x, y, sem_in, sem_out):
    parts = [
        (arrays, pl.ds(32 * half, 32), 2 * half + n)
        for half in range(2)
        for n, arrays in enumerate(((a_hbm, a, x, x_hbm), (b_hbm, b, y, y_hbm)))
    ]
    ins = [pltpu.make_async_copy(r[0].at[p], r[1].at[p], sem_in.at[k]) for r, p, k in parts]
    outs = [pltpu.make_async_copy(r[2].at[p], r[3].at[p], sem_out.at[k]) for r, p, k in parts]
    for c in ins:
        c.start()
    for c, out, (r, p, _) in zip(ins, outs, parts):
        c.wait()
        r[2][p] = r[1][p]
        out.start()
    for out in outs:
        out.wait()


def on_device(volume, cotangent, gain_width, qkv_width, out_width, gain_height, qkv_height, out_height):
    shape = volume.shape
    hbm = pl.BlockSpec(memory_space=pl.ANY)
    flat = jax.ShapeDtypeStruct((64, 4, D), BF)
    v = lambda *s: pltpu.VMEM(s, BF)
    result, grad = pl.pallas_call(
        kernel,
        out_shape=(flat, flat),
        in_specs=[hbm] * 8,
        out_specs=(hbm, hbm),
        scratch_shapes=[
            v(64, 4, D), v(64, 4, D), v(64, 4, D), v(64, 4, D), v(D), v(D), v(D, 3 * INNER), v(INNER, D), v(D, 3 * INNER), v(INNER, D), v(4, TOK, TOK), v(128, 128),
            v(2, 32, 8, 512), v(2, 32, 8, 512), v(2, 64, 8, 128), v(2, 64, 8, 128),
            v(64, 16, 128), v(64, 16, 128), v(2, 32, 8, 512), v(2, 32, 8, 512),
            v(16, 2, 8, D), v(2, 2, 8, 8, D), v(16, 2, 8, D), v(2, 2, 8, 8, D),
            v(2, 2, 8, 8, D), v(16, 2, 8, D), v(2, 2, 8, 8, D), v(16, 2, 8, D),
            v(TOK, 3 * INNER), v(TOK, 3 * INNER), pltpu.VMEM((8, TOK, 128), F32), pltpu.VMEM((8, TOK, 128), F32),
            v(TOK, INNER), v(TOK, INNER), v(TOK, 3 * INNER), v(TOK, INNER), v(TOK, INNER), v(TOK, D),
            pltpu.SemaphoreType.DMA((8,)), pltpu.SemaphoreType.DMA((2,)), pltpu.SemaphoreType.DMA((12,)), pltpu.SemaphoreType.DMA((12,)),
            pltpu.SemaphoreType.DMA,
        ],
        compiler_params=pltpu.CompilerParams(
            collective_id=0, has_side_effects=True, vmem_limit_bytes=60 * 1024 * 1024
        ),
    )(
        volume.reshape(64, 4, D), cotangent.reshape(64, 4, D), gain_width, gain_height,
        qkv_width, out_width, qkv_height, out_height,
    )
    result, grad = pl.pallas_call(
        hand_over,
        out_shape=(flat, flat),
        in_specs=[hbm, hbm],
        out_specs=(hbm, hbm),
        scratch_shapes=[v(64, 4, D)] * 4 + [pltpu.SemaphoreType.DMA((4,))] * 2,
    )(result, grad)
    return result.reshape(shape), grad.reshape(shape)


def solution(mesh):
    split = P(None, "outer", "inner", None)
    return jax.shard_map(
        on_device,
        mesh=mesh,
        in_specs=(split, split, P(), P(), P(), P(), P(), P()),
        out_specs=(split, split),
        check_vma=False,
    )
```

```python
import jax
import jax.numpy as jnp
from jax import lax
from jax.experimental import pallas as pl
from jax.experimental.pallas import tpu as pltpu
from jax.sharding import PartitionSpec as P

MESH = pl.DeviceIdType.MESH
BF = jnp.bfloat16
F32 = jnp.float32
D = 1024
INNER = 512
NI = 32
NO = 8
TOK = 256
PAIRS = 4
EPS = 1e-06


def dot(a, b):
    return jnp.dot(a, b, preferred_element_type=F32)


def dot_nt(a, b):
    return lax.dot_general(a, b, (((1,), (1,)), ((), ())), preferred_element_type=F32)


def dot_tn(a, b):
    return lax.dot_general(a, b, (((0,), (0,)), ((), ())), preferred_element_type=F32)


def home_to_height(r):
    return (r // 64) * 64 + ((r % 8) * 2 + (r // 8) % 2) * 4 + (r // 16) % 4


def height_to_home(r):
    return (r // 64) * 64 + (r % 4) * 16 + ((r // 4) % 2) * 8 + (r // 8) % 8


def last_to_first(r):
    return (r % 64) * 2 + r // 64


def back_to_lines(r):
    return ((r // 2) % 64) * 4 + (r // 128) * 2 + r % 2


def lines_to_back(r):
    return (r % 2) * 128 + ((r // 2) % 2) * 64 + r // 4


def one_hot(order, n):
    row = lax.broadcasted_iota(jnp.int32, (n, n), 0)
    col = lax.broadcasted_iota(jnp.int32, (n, n), 1)
    return jnp.where(col == order(row), 1.0, 0.0).astype(BF)


def in_low(shape, size):
    return (lax.broadcasted_iota(jnp.int32, shape, 1) // size) % 2 == 0


def swap(a, b, size):
    low = in_low(a.shape, size)
    return jnp.where(low, a, pltpu.roll(b, size, 1)), jnp.where(low, pltpu.roll(a, 8 - size, 1), b)


def pack_tokens(rows):
    g = rows.reshape(rows.shape[0] // 8, 8, D)
    return swap(g[:, :, : D // 2], g[:, :, D // 2 :], 4)


def unpack_tokens(a, b):
    a, b = swap(a, b, 4)
    return jnp.concatenate([a, b], axis=2).reshape(a.shape[0] * 8, D)


def turn(q):
    a0, a2 = swap(q[0], q[2], 4)
    a1, a3 = swap(q[1], q[3], 4)
    return swap(a0, a1, 2) + swap(a2, a3, 2)


def pack_pairs(rows):
    g = rows.reshape(16, 8, INNER)
    parts = turn([g[:, :, 128 * q : 128 * q + 128] for q in range(4)])
    return jnp.stack(parts, axis=1).reshape(64, 8, 128).astype(BF)


def unpack_pairs(blocks):
    g = blocks.astype(F32).reshape(16, 4, 8, 128)
    return jnp.concatenate(turn([g[:, q] for q in range(4)]), axis=2).reshape(128, INNER).astype(BF)


def pack_fours(rows):
    g = rows.reshape(32, 8, INNER)
    q = [g[:, :, 128 * k : 128 * k + 128] for k in range(4)]
    (a0, b0), (a1, b1) = swap(q[0], q[1], 4), swap(q[2], q[3], 4)
    return jnp.stack((a0, a1, b0, b1), axis=1).reshape(64, 16, 128).astype(BF)


def unpack_fours(blocks):
    g = blocks.astype(F32).reshape(32, 4, 8, 128)
    parts = swap(g[:, 0], g[:, 2], 4) + swap(g[:, 1], g[:, 3], 4)
    return jnp.concatenate(parts, axis=2).reshape(TOK, INNER).astype(BF)


def scale_of(v):
    return lax.rsqrt(jnp.mean(v * v, axis=-1, keepdims=True) + EPS)


def norm_back(v, dn, gain, resid):
    r = scale_of(v)
    gd = dn * gain
    c = jnp.sum(gd * v, axis=-1, keepdims=True) * (1.0 / D)
    return r * gd - v * (r * r * r * c) + resid


def lane_low():
    return lax.broadcasted_iota(jnp.int32, (128, 128), 1) < 64


def two_heads(a):
    low = lane_low()
    zero = jnp.zeros_like(a)
    return jnp.concatenate([jnp.where(low, a, zero), jnp.where(low, zero, a)], axis=0)


def one_pair(a):
    return jnp.where(lane_low(), a[:128], a[128:])


def unit_slices(line, pair):
    rows = pl.ds(line * 128, 128)
    return rows, [pl.ds(INNER * part + 128 * pair, 128) for part in range(3)]


def attend(proj, probs, mixed, line):
    for pair in range(PAIRS):
        rows, (qs, ks, vs) = unit_slices(line, pair)
        s = dot_nt(two_heads(proj[rows, qs]), proj[rows, ks]) * 0.125
        e = jnp.exp(s - jnp.max(s, axis=-1, keepdims=True))
        p = e * (1.0 / jnp.sum(e, axis=-1, keepdims=True))
        probs[line * PAIRS + pair] = p
        mixed[rows, pl.ds(128 * pair, 128)] = one_pair(dot(p.astype(BF), proj[rows, vs])).astype(BF)


def attend_back(proj, probs, dmixed, dproj, line):
    for pair in range(PAIRS):
        rows, (qs, ks, vs) = unit_slices(line, pair)
        p = probs[line * PAIRS + pair]
        do = two_heads(dmixed[rows, pl.ds(128 * pair, 128)])
        dp = dot_nt(do, proj[rows, vs]).astype(BF).astype(F32)
        dproj[rows, vs] = dot_tn(p.astype(BF), do).astype(BF)
        ds = p * (dp - jnp.sum(dp * p, axis=-1, keepdims=True)) * 0.125
        ds = ds.astype(BF)
        dproj[rows, qs] = one_pair(dot(ds, proj[rows, ks])).astype(BF)
        dproj[rows, ks] = dot_tn(ds, two_heads(proj[rows, qs])).astype(BF)


FAR_FIRST = (4, 3, 5, 2, 6, 1, 7, 0)


def kernel(
    vol_hbm, cot_hbm, gw_hbm, gh_hbm, qkvw_hbm, outw_hbm, qkvh_hbm, outh_hbm,
    res_hbm, grad_hbm,
    vol_ref, cot_ref, res_ref, grad_ref, gw_ref, gh_ref, qkvw, outw, qkvh, outh, perms, halves,
    s1, r1, s2, r2, s3, r3, s4, r4,
    sx, rx, sc, rc, sres, rres, smg, rmg,
    proj, projh, probs, probsh, mixed, mixedh, dproj, dmix, dmixh, mid,
    load_sem, store_sem, send_sem, recv_sem, local_sem,
):
    i = lax.axis_index("inner")
    o = lax.axis_index("outer")
    ix, iz, ic = i // 16, (i // 2) % 8, i % 2
    oy, ol = o // 2, o % 2
    frame_w = (iz % 2) * 2 + ix
    slot_w = (iz // 2) * 2 + ic
    frame_h = (oy + iz) % 4
    same = frame_w == frame_h
    xs = (ix, (ix + 1) % 2)
    zs = [(iz + d) % 8 for d in range(8)]
    cs = (ic, (ic + 1) % 2)

    barrier = pltpu.get_barrier_semaphore()
    for dx in (1, 0):
        for dz in FAR_FIRST:
            for dc in (1, 0):
                if dx or dz or dc:
                    greeted = {"inner": xs[dx] * 16 + zs[dz] * 2 + cs[dc]}
                    pl.semaphore_signal(barrier, inc=1, device_id=greeted, device_id_type=MESH)
    for dp in range(1, NO):
        pl.semaphore_signal(barrier, inc=1, device_id={"outer": (o + dp) % NO}, device_id_type=MESH)

    moves = ((vol_hbm, vol_ref), (cot_hbm, cot_ref), (qkvw_hbm, qkvw), (outh_hbm, outh), (outw_hbm, outw), (qkvh_hbm, qkvh), (gw_hbm, gw_ref), (gh_hbm, gh_ref))
    loads = [pltpu.make_async_copy(a, b, load_sem.at[n]) for n, (a, b) in enumerate(moves)]
    for n in (0, 6, 7, 1, 2, 3, 4, 5):
        loads[n].start()

    def remote(src, dst, sem, target):
        pltpu.make_async_remote_copy(
            src_ref=src, dst_ref=dst, send_sem=send_sem.at[sem], recv_sem=recv_sem.at[sem],
            device_id=target, device_id_type=MESH,
        ).start()

    def local(src, dst):
        copy = pltpu.make_async_copy(src, dst, local_sem)
        copy.start()
        copy.wait()

    def block(x, z, c):
        return ((z % 2) * 2 + x) * 8 + (z // 2) * 2 + c

    def to_width():
        for odd in (0, 1):
            turned = (iz + odd) % 2
            far = [(iz + a + turned * (b - a)) % 8 for a, b in ((4, 3), (2, 5), (6, 1), (0, 7))]
            for half in (0, 1):
                for dx in (1, 0):
                    for k, z in enumerate(far):
                        for dc in (1, 0):
                            x, c = xs[dx], cs[dc]
                            src, dst = s1.at[half, block(x, z, c)], r1.at[half, i]
                            send = lambda src=src, dst=dst, d=x * 16 + z * 2 + c, half=half: remote(src, dst, half, {"inner": d})
                            if dx or dc or k < 3:
                                send()
                            else:
                                pl.when(turned != 0)(send)
                                pl.when(turned == 0)(lambda src=src, dst=dst: local(src, dst))

    def from_width(half):
        for dx in (1, 0):
            for dz in FAR_FIRST:
                for dc in (1, 0):
                    d = xs[dx] * 16 + zs[dz] * 2 + cs[dc]
                    src, dst = s4.at[half, d], r4.at[half, block(ix, iz, ic)]
                    if dx or dz or dc:
                        remote(src, dst, 6 + half, {"inner": d})
                    else:
                        local(src, dst)

    def width_to_height(half):
        for dx in (1, 0):
            for dz in FAR_FIRST:
                y = (frame_w + 8 - zs[dz]) % 4
                for dc in (1, 0):
                    for e in (0, 1):
                        s = xs[dx] * 16 + zs[dz] * 2 + cs[dc]
                        p = y * 2 + e
                        src, dst = s2.at[half, 2 * s + e], r2.at[half, o * 8 + slot_w]
                        if dx or dz or dc:
                            remote(src, dst, 2 + half, {"outer": p, "inner": s})
                        else:
                            pl.when(p != o)(lambda src=src, dst=dst, p=p, s=s: remote(src, dst, 2 + half, {"outer": p, "inner": s}))
                            pl.when(p == o)(lambda src=src, dst=dst: local(src, dst))

    def height_to_width():
        base = (frame_h % 2) * 16 + (frame_h // 2) * 2
        js = [(slot_w + k) % 8 for k in range(8)]
        ds = [base + (j // 2) * 4 + j % 2 for j in js]
        for dp in (7, 6, 5, 4, 3, 2, 1, 0):
            p = (o + dp) % 8
            for k in range(8):
                src, dst = s3.at[p * 8 + js[k]], r3.at[2 * i + ol]
                if dp or k:
                    remote(src, dst, 4, {"outer": p, "inner": ds[k]})
                else:
                    pl.when(ds[k] != i)(lambda src=src, dst=dst, p=p, d=ds[k]: remote(src, dst, 4, {"outer": p, "inner": d}))
                    pl.when(ds[k] == i)(lambda src=src, dst=dst: local(src, dst))

    def height_line(p):
        return 2 * ((p // 2 + iz) % 4) + p % 2

    def to_height(src, dst, sem):
        def go(k, c):
            p = (o + k) % NO
            remote(src.at[pl.ds(height_line(p) * 2, 2)], dst.at[:, :, o], sem, {"outer": p})
            return c

        lax.fori_loop(1, NO, go, 0)
        local(src.at[pl.ds(height_line(o) * 2, 2)], dst.at[:, :, o])

    def from_height(src, dst, sem):
        def go(k, c):
            p = (o + k) % NO
            remote(src.at[:, :, p], dst.at[pl.ds(height_line(o) * 2, 2)], sem, {"outer": p})
            return c

        lax.fori_loop(1, NO, go, 0)
        local(src.at[:, :, o], dst.at[pl.ds(height_line(o) * 2, 2)])

    def wait_bytes(part, sem):
        pltpu.make_async_copy(part, part, sem).wait()

    def wait_inner(buf, half, sem):
        wait_bytes(buf.at[half, pl.ds(0, 31)], sem)

    def wait_back(buf, sem):
        pl.when(same)(lambda: wait_bytes(buf.at[pl.ds(0, 63)], sem))
        pl.when(jnp.logical_not(same))(lambda: wait_bytes(buf, sem))

    def wait_cross(buf, half, sem):
        pl.when(same)(lambda: wait_bytes(buf.at[half, pl.ds(0, 63)], sem))
        pl.when(jnp.logical_not(same))(lambda: wait_bytes(buf.at[half], sem))

    def wait_lines(buf, sem):
        wait_bytes(buf.at[:, :, pl.ds(0, 7)], sem)

    def wait_home(buf, sem):
        wait_bytes(buf.at[pl.ds(0, 14)], sem)

    loads[6].wait()
    loads[7].wait()
    gain_w = gw_ref[...].astype(F32).reshape(1, D)
    gain_h = gh_ref[...].astype(F32).reshape(1, D)
    loads[0].wait()
    x = vol_ref[...].astype(F32).reshape(TOK, D)
    first, second = pack_tokens(x * scale_of(x) * gain_w)
    s1[0] = first.astype(BF)
    s1[1] = second.astype(BF)
    pl.semaphore_wait(barrier, NI + NO - 2)
    to_width()

    perms[0] = one_hot(home_to_height, TOK)
    sx[...] = dot(perms[0], x.astype(BF)).astype(BF).reshape(16, 2, 8, D)
    to_height(sx, rx, 8)
    loads[1].wait()
    cot = cot_ref[...].astype(F32).reshape(TOK, D).astype(BF)
    sc[...] = dot(perms[0], cot).astype(BF).reshape(16, 2, 8, D)
    to_height(sc, rc, 9)
    perms[1] = one_hot(height_to_home, TOK)
    perms[2] = one_hot(back_to_lines, TOK)
    halves[...] = one_hot(last_to_first, 128)
    perms[3] = one_hot(lines_to_back, TOK)
    loads[2].wait()
    loads[3].wait()

    wait_inner(r1, 0, recv_sem.at[0])
    wait_inner(r1, 1, recv_sem.at[1])
    got = r1[...].astype(F32).reshape(32, 2, 8, D // 2)
    tokens = unpack_tokens(got[:, 0], got[:, 1]).astype(BF)
    proj[...] = dot(tokens, qkvw[...]).astype(BF)
    for line in range(2):
        attend(proj, probs, mixed, line)
        s2[line] = pack_pairs(mixed[pl.ds(line * 128, 128)].astype(F32))
        width_to_height(line)

    loads[4].wait()
    loads[5].wait()
    wait_lines(rx, recv_sem.at[8])
    wait_lines(rc, recv_sem.at[9])
    dmixh[...] = dot_nt(rc[...].reshape(TOK, D), outh[...]).astype(BF)

    for half in range(2):
        wait_cross(r2, half, recv_sem.at[2 + half])
        here = dot(halves[...], unpack_pairs(r2[half])).astype(BF)
        middle = (rx[:, half].astype(F32).reshape(128, D) + dot(here, outw[...])).astype(BF)
        m32 = middle.astype(F32)
        normed = (m32 * scale_of(m32) * gain_h).astype(BF)
        got = dot(normed, qkvh[...]).astype(BF)
        for line in range(2):
            rows = pl.ds(line * 128 + half * 64, 64)
            mid[rows] = middle[line * 64 : line * 64 + 64]
            projh[rows] = got[line * 64 : line * 64 + 64]
    for line in range(2):
        attend(projh, probsh, mixedh, line)
        attend_back(projh, probsh, dmixh, dproj, line)
    dn = dot_nt(dproj[...], qkvh[...]).astype(BF).astype(F32)
    mgrad = norm_back(mid[...].astype(F32), dn, gain_h, rc[...].astype(F32).reshape(TOK, D)).astype(BF)
    smg[...] = mgrad.reshape(2, 2, 8, 8, D)
    dmw = dot_nt(mgrad, outw[...]).astype(BF)
    s3[...] = pack_fours(dot(perms[3], dmw))
    height_to_width()
    from_height(smg, rmg, 10)
    sres[...] = (mid[...].astype(F32) + dot(mixedh[...], outh[...])).astype(BF).reshape(2, 2, 8, 8, D)
    from_height(sres, rres, 11)

    wait_back(r3, recv_sem.at[4])
    dmix[...] = dot(perms[2], unpack_fours(r3[...])).astype(BF)
    for line in range(2):
        rows = pl.ds(line * 128, 128)
        attend_back(proj, probs, dmix, dproj, line)
        dn = dot_nt(dproj[rows], qkvw[...]).astype(BF).astype(F32)
        s4[line] = jnp.stack(pack_tokens(dn), axis=1).reshape(NI, 8, D // 2).astype(BF)
        from_width(line)

    wait_home(rres, recv_sem.at[11])
    res_ref[...] = dot(perms[1], rres[...].reshape(TOK, D)).reshape(64, 4, D).astype(BF)
    stores = [
        pltpu.make_async_copy(a, b, store_sem.at[n])
        for n, (a, b) in enumerate(((res_ref, res_hbm), (grad_ref, grad_hbm)))
    ]
    stores[0].start()
    wait_home(rmg, recv_sem.at[10])
    resid = dot(perms[1], rmg[...].reshape(TOK, D))
    wait_inner(r4, 0, recv_sem.at[6])
    wait_inner(r4, 1, recv_sem.at[7])
    x = vol_ref[...].astype(F32).reshape(TOK, D)
    dn = unpack_tokens(r4[0].astype(F32), r4[1].astype(F32))
    grad_ref[...] = norm_back(x, dn, gain_w, resid).reshape(64, 4, D).astype(BF)
    stores[1].start()

    for half in range(2):
        wait_inner(s1, half, send_sem.at[half])
        wait_cross(s2, half, send_sem.at[2 + half])
        wait_inner(s4, half, send_sem.at[6 + half])
    wait_back(s3, send_sem.at[4])
    wait_home(sx, send_sem.at[8])
    wait_home(sc, send_sem.at[9])
    wait_lines(smg, send_sem.at[10])
    wait_lines(sres, send_sem.at[11])
    stores[0].wait()
    stores[1].wait()


def hand_over(a_hbm, b_hbm, x_hbm, y_hbm, a, b, x, y, sem_in, sem_out):
    parts = [
        (arrays, pl.ds(32 * half, 32), 2 * half + n)
        for half in range(2)
        for n, arrays in enumerate(((a_hbm, a, x, x_hbm), (b_hbm, b, y, y_hbm)))
    ]
    ins = [pltpu.make_async_copy(r[0].at[p], r[1].at[p], sem_in.at[k]) for r, p, k in parts]
    outs = [pltpu.make_async_copy(r[2].at[p], r[3].at[p], sem_out.at[k]) for r, p, k in parts]
    for c in ins:
        c.start()
    for c, out, (r, p, _) in zip(ins, outs, parts):
        c.wait()
        r[2][p] = r[1][p]
        out.start()
    for out in outs:
        out.wait()


def on_device(volume, cotangent, gain_width, qkv_width, out_width, gain_height, qkv_height, out_height):
    shape = volume.shape
    hbm = pl.BlockSpec(memory_space=pl.ANY)
    flat = jax.ShapeDtypeStruct((64, 4, D), BF)
    v = lambda *s: pltpu.VMEM(s, BF)
    result, grad = pl.pallas_call(
        kernel,
        out_shape=(flat, flat),
        in_specs=[hbm] * 8,
        out_specs=(hbm, hbm),
        scratch_shapes=[
            v(64, 4, D), v(64, 4, D), v(64, 4, D), v(64, 4, D), v(D), v(D), v(D, 3 * INNER), v(INNER, D), v(D, 3 * INNER), v(INNER, D), v(4, TOK, TOK), v(128, 128),
            v(2, 32, 8, 512), v(2, 32, 8, 512), v(2, 64, 8, 128), v(2, 64, 8, 128),
            v(64, 16, 128), v(64, 16, 128), v(2, 32, 8, 512), v(2, 32, 8, 512),
            v(16, 2, 8, D), v(2, 2, 8, 8, D), v(16, 2, 8, D), v(2, 2, 8, 8, D),
            v(2, 2, 8, 8, D), v(16, 2, 8, D), v(2, 2, 8, 8, D), v(16, 2, 8, D),
            v(TOK, 3 * INNER), v(TOK, 3 * INNER), pltpu.VMEM((8, TOK, 128), F32), pltpu.VMEM((8, TOK, 128), F32),
            v(TOK, INNER), v(TOK, INNER), v(TOK, 3 * INNER), v(TOK, INNER), v(TOK, INNER), v(TOK, D),
            pltpu.SemaphoreType.DMA((8,)), pltpu.SemaphoreType.DMA((2,)), pltpu.SemaphoreType.DMA((12,)), pltpu.SemaphoreType.DMA((12,)),
            pltpu.SemaphoreType.DMA,
        ],
        compiler_params=pltpu.CompilerParams(
            collective_id=0, has_side_effects=True, vmem_limit_bytes=60 * 1024 * 1024
        ),
    )(
        volume.reshape(64, 4, D), cotangent.reshape(64, 4, D), gain_width, gain_height,
        qkv_width, out_width, qkv_height, out_height,
    )
    result, grad = pl.pallas_call(
        hand_over,
        out_shape=(flat, flat),
        in_specs=[hbm, hbm],
        out_specs=(hbm, hbm),
        scratch_shapes=[v(64, 4, D)] * 4 + [pltpu.SemaphoreType.DMA((4,))] * 2,
    )(result, grad)
    return result.reshape(shape), grad.reshape(shape)


def solution(mesh):
    split = P(None, "outer", "inner", None)
    return jax.shard_map(
        on_device,
        mesh=mesh,
        in_specs=(split, split, P(), P(), P(), P(), P(), P()),
        out_specs=(split, split),
        check_vma=False,
    )
```
